512 devices in a mesh: train: 32 (over z_lo, y, core), col: 16 (over x, z_hi).
Axes of the slice: x: 4, y: 4, z: 16 (z_hi: 4, z_lo: 4; z = z_hi * 4 + z_lo), core: 2. Of those that a mesh axis runs over, the one named last changes fastest.
Arguments:
- train_grads: bfloat16 [32768, 32768], P('train', 'col'), may hold values from -0.03125 to 0.03125
- test_grads: bfloat16 [1024, 32768], P('train', 'col'), may hold values from -6 to 6
- precond: bfloat16 [256, 128, 128], P('col'), may hold values from -2 to 4
Outputs:
- scores: bfloat16 [1024, 32768], P('col', 'train')
The draws below stay inside these ranges and needn't reach their ends.
All inputs are finite; a program needn't handle non-finite values.
Results may differ from the reference program's by a relative error of at most 0.0049.
Values may be sent and summed in bfloat16 or wider, within the bound.
No kernel may reach another device: no remote copies, remote signals or barrier semaphores. Data moves between devices by JAX's collectives and lax.ppermute only.
A program may use at most 64 MiB of HBM per device.

```python
import jax
import jax.numpy as jnp
from jax import lax

K = 32768
BLOCK = 128
TRAIN_DEV = 1024
TEST = 1024
NTRAIN = 32768
NBLK = 256
N_TRAIN = 32


def draw_precond(key, part):
    key = jax.random.fold_in(key, 7)
    first, second = jax.random.split(key)
    rows = lax.broadcasted_iota(jnp.int32, (NBLK, BLOCK, BLOCK), 1)
    cols = lax.broadcasted_iota(jnp.int32, (NBLK, BLOCK, BLOCK), 2)
    eye = (rows == cols).astype(jnp.float32)
    raw = jnp.clip(jax.random.normal(first, (NBLK, BLOCK, BLOCK), jnp.float32), -3.0, 3.0)
    level = jax.random.uniform(second, (NBLK, 1, BLOCK), jnp.float32, -0.69, 0.69)
    diag = jnp.exp(level)
    off = 0.25 * (raw + jnp.swapaxes(raw, 1, 2)) / jnp.sqrt(jnp.float32(BLOCK))
    result = eye * diag + (1.0 - eye) * off
    return result.astype(jnp.bfloat16)


def shard_levels(own_key, shape, cuts, smallest, top_value):
    loudness = 1.0
    for position, parts in cuts:
        steps = jax.random.uniform(jax.random.fold_in(jax.random.fold_in(own_key, 6), position), (parts,), jnp.float32, smallest / len(cuts), top_value / len(cuts))
        loudness = loudness * jnp.repeat(jnp.exp(steps), shape[position] // parts).reshape((-1,) + (1,) * (len(shape) - 1 - position))
    return loudness


def noise(rng, extent, width, limit, cuts=(), dtype=jnp.bfloat16):
    values = width * jax.random.normal(rng, extent, jnp.float32)
    if cuts:
        values = values * shard_levels(rng, extent, cuts, -0.22, 0.18)
    return jnp.clip(values, -limit, limit).astype(dtype)


def setup_inputs(seed: int = 0) -> dict:
    keys = jax.random.split(jax.random.key(seed), 4)
    train_grads = noise(keys[0], (NTRAIN, K), K ** -0.5, 0.03125, ((0, 32), (1, 16)))
    test_grads = noise(keys[1], (TEST, K), 1.0, 6.0, ((0, 32), (1, 16)))
    precond = draw_precond(jax.random.fold_in(keys[3], 71), 0)
    return dict(train_grads=train_grads, test_grads=test_grads, precond=precond)


def reference(train_grads, test_grads, precond):
    shaped = test_grads.astype(jnp.float32).reshape(TEST, NBLK, BLOCK)
    conditioned = jnp.einsum("tbi,bij->tbj", shaped, precond.astype(jnp.float32))
    conditioned = conditioned.reshape(TEST, K).astype(jnp.bfloat16)
    blocked = train_grads.reshape(N_TRAIN, TRAIN_DEV, K)

    def score_block(rows):
        return jnp.dot(conditioned, rows.T, preferred_element_type=jnp.float32)

    result = lax.map(score_block, blocked)
    result = jnp.transpose(result, (1, 0, 2)).reshape(TEST, NTRAIN)
    return result.astype(jnp.bfloat16)
```

```python
import jax
import jax.numpy as jnp
import numpy as np
from jax import lax
from jax.experimental import pallas as pl
from jax.experimental.pallas import tpu as pltpu
from jax.sharding import Mesh, PartitionSpec as P

AXES = ("zl", "y", "core", "x", "zh")
SIZES = (4, 4, 2, 4, 4)
BLOCK = 128


def condition_kernel(rows_ref, precond_ref, out_ref):
    for b in range(precond_ref.shape[0]):
        cols = pl.ds(b * BLOCK, BLOCK)
        out_ref[:, cols] = jnp.dot(
            rows_ref[:, cols], precond_ref[b], preferred_element_type=jnp.float32
        ).astype(out_ref.dtype)


def condition(rows, precond):
    return pl.pallas_call(
        condition_kernel,
        out_shape=jax.ShapeDtypeStruct(rows.shape, rows.dtype),
        in_specs=[pl.BlockSpec(memory_space=pltpu.VMEM)] * 2,
        out_specs=pl.BlockSpec(memory_space=pltpu.VMEM),
    )(rows, precond)


def shift(array, axis, step):
    size = SIZES[AXES.index(axis)]
    return lax.ppermute(array, axis, [(i, (i + step) % size) for i in range(size)])


def dot_t(rows, train):
    out = lax.dot_general(
        rows, train, (((1,), (1,)), ((), ())), preferred_element_type=jnp.float32
    )
    return out.astype(jnp.bfloat16)


def f32_sum(arrays):
    total = arrays[0].astype(jnp.float32)
    for a in arrays[1:]:
        total = total + a.astype(jnp.float32)
    return total


def per_device(train_grads, test_grads, precond):
    zl, y, core = lax.axis_index("zl"), lax.axis_index("y"), lax.axis_index("core")
    x, zh = lax.axis_index("x"), lax.axis_index("zh")
    count = test_grads.shape[0]
    width = train_grads.shape[0]

    own = condition(test_grads, precond)
    line = jnp.concatenate([own] + [shift(own, "zl", k) for k in (1, 2, 3)], axis=0)
    plane = jnp.concatenate([line] + [shift(line, "y", m) for m in (1, 2, 3)], axis=0)
    other = shift(plane, "core", 1)

    shape = (4, 4, count, width)
    part = [dot_t(plane, train_grads).reshape(shape), dot_t(other, train_grads).reshape(shape)]

    def for_x(step):
        k = jnp.mod(zl - x - step, 4)
        return jnp.stack(
            [lax.dynamic_index_in_dim(p, k, axis=1, keepdims=False) for p in part], axis=1
        )

    got = [for_x(0)] + [shift(for_x(j), "x", j) for j in (1, 2, 3)]
    total = f32_sum(got)

    def for_zh(step):
        m = jnp.mod(y - zh - step, 4)
        return lax.dynamic_index_in_dim(total, m, axis=0, keepdims=False)

    last = [for_zh(0)] + [shift(for_zh(i).astype(jnp.bfloat16), "zh", i) for i in (1, 2, 3)]
    scores = f32_sum(last).astype(jnp.bfloat16)
    scores = jnp.where(core == 0, scores, scores[::-1])
    return scores.reshape(2 * count, width)


def solution(mesh):
    fine = Mesh(mesh.devices.reshape(SIZES), AXES)
    train, col = ("zl", "y", "core"), ("x", "zh")
    return jax.shard_map(
        per_device,
        mesh=fine,
        in_specs=(P(train, col), P(train, col), P(col, None, None)),
        out_specs=P(col, train),
        check_vma=False,
    )
```

```python
import jax
import jax.numpy as jnp
from jax import lax
from jax.experimental import pallas as pl
from jax.experimental.pallas import tpu as pltpu
from jax.sharding import Mesh, PartitionSpec as P

AXES = ("zl", "y", "core", "x", "zh")
SIZES = (4, 4, 2, 4, 4)
BLOCK = 128


def condition_kernel(rows_ref, precond_ref, out_ref):
    for b in range(precond_ref.shape[0]):
        cols = pl.ds(b * BLOCK, BLOCK)
        out_ref[:, cols] = jnp.dot(
            rows_ref[:, cols], precond_ref[b], preferred_element_type=jnp.float32
        ).astype(out_ref.dtype)


def condition(rows, precond):
    return pl.pallas_call(
        condition_kernel,
        out_shape=jax.ShapeDtypeStruct(rows.shape, rows.dtype),
        in_specs=[pl.BlockSpec(memory_space=pltpu.VMEM)] * 2,
        out_specs=pl.BlockSpec(memory_space=pltpu.VMEM),
    )(rows, precond)


def shift(array, axis, step):
    size = SIZES[AXES.index(axis)]
    return lax.ppermute(array, axis, [(i, (i + step) % size) for i in range(size)])


def dot_t(rows, train):
    out = lax.dot_general(
        rows, train, (((1,), (1,)), ((), ())), preferred_element_type=jnp.float32
    )
    return out.astype(jnp.bfloat16)


def halve_x(array, first):
    pairs = []
    for core in range(2):
        for x in range(4):
            up = (x + core + (0 if first else 1)) % 2 == 0
            pairs.append((core * 4 + x, core * 4 + (x + (1 if up else 3)) % 4))
    return lax.ppermute(array, ("core", "x"), pairs)


def per_device(train_grads, test_grads, precond):
    zl, y, core = lax.axis_index("zl"), lax.axis_index("y"), lax.axis_index("core")
    x, zh = lax.axis_index("x"), lax.axis_index("zh")
    count = test_grads.shape[0]
    width = train_grads.shape[0]

    own = condition(test_grads, precond)
    near = {k: shift(own, "zl", k) for k in (2, 1, 3)}
    own_y = {m: shift(own, "y", m) for m in (2, 1, 3)}
    near, own_y = lax.optimization_barrier((near, own_y))
    rest = jnp.concatenate([near[k] for k in (1, 2, 3)], axis=0)
    rest_y = {m: shift(rest, "y", m) for m in (2, 1, 3)}
    plane = [own, rest]
    for m in (1, 2, 3):
        plane += [own_y[m], rest_y[m]]
    plane = jnp.concatenate(plane, axis=0)
    other = shift(plane, "core", 1)

    shape = (4, 4, count, width)
    part = [dot_t(plane, train_grads).reshape(shape), dot_t(other, train_grads).reshape(shape)]

    first = jnp.where(jnp.mod(x + core, 2) == 0, 1, 3)

    def block(i, j):
        m, k = jnp.mod(y - zh - i, 4), jnp.mod(zl - x - j, 4)
        return jnp.concatenate(
            [lax.dynamic_slice(p, (m, k, 0, 0), (1, 1, count, width))[0] for p in part], axis=0
        )

    def sum_x(i):
        send = jnp.concatenate([block(i, first), block(i, 2)], axis=0)
        got = halve_x(send, True)
        keep = block(i, 0).astype(jnp.float32) + got[:2].astype(jnp.float32)
        back = block(i, 4 - first).astype(jnp.float32) + got[2:].astype(jnp.float32)
        return keep + halve_x(back.astype(jnp.bfloat16), False).astype(jnp.float32)

    sums = {i: sum_x(i) for i in (2, 1, 3, 0)}
    total = sums[0]
    for i in (2, 1, 3):
        total = total + shift(sums[i].astype(jnp.bfloat16), "zh", i).astype(jnp.float32)
    scores = total.astype(jnp.bfloat16)
    scores = jnp.where(core == 0, scores, scores[::-1])
    return scores.reshape(2 * count, width)


def solution(mesh):
    fine = Mesh(mesh.devices.reshape(SIZES), AXES)
    train, col = ("zl", "y", "core"), ("x", "zh")
    return jax.shard_map(
        per_device,
        mesh=fine,
        in_specs=(P(train, col), P(train, col), P(col, None, None)),
        out_specs=P(col, train),
        check_vma=False,
    )
```

```python
import jax
import jax.numpy as jnp
from jax import lax
from jax.experimental import pallas as pl
from jax.experimental.pallas import tpu as pltpu
from jax.sharding import Mesh, PartitionSpec as P

AXES = ("zl", "y", "core", "x", "zh")
SIZES = (4, 4, 2, 4, 4)
BLOCK = 128


def condition_kernel(rows_ref, precond_ref, out_ref):
    for b in range(precond_ref.shape[0]):
        cols = pl.ds(b * BLOCK, BLOCK)
        out_ref[:, cols] = jnp.dot(
            rows_ref[:, cols], precond_ref[b], preferred_element_type=jnp.float32
        ).astype(out_ref.dtype)


def condition(rows, precond):
    return pl.pallas_call(
        condition_kernel,
        out_shape=jax.ShapeDtypeStruct(rows.shape, rows.dtype),
        in_specs=[pl.BlockSpec(memory_space=pltpu.VMEM)] * 2,
        out_specs=pl.BlockSpec(memory_space=pltpu.VMEM),
    )(rows, precond)


def shift(array, axis, step):
    size = SIZES[AXES.index(axis)]
    return lax.ppermute(array, axis, [(i, (i + step) % size) for i in range(size)])


def dot_t(rows, train):
    out = lax.dot_general(
        rows, train, (((1,), (1,)), ((), ())), preferred_element_type=jnp.float32
    )
    return out.astype(jnp.bfloat16)


def halve(array, axis, first):
    names = {"y": ("y", "core"), "x": ("core", "x"), "zh": ("core", "zh")}[axis]
    pairs = []
    for core in range(2):
        for i in range(4):
            up = (i + core + (0 if first else 1)) % 2 == 0
            to = (i + (1 if up else 3)) % 4
            if axis == "y":
                pairs.append((i * 2 + core, to * 2 + core))
            else:
                pairs.append((core * 4 + i, core * 4 + to))
    return lax.ppermute(array, names, pairs)


def first_step(index, core):
    return jnp.where(jnp.mod(index + core, 2) == 0, 1, 3)


def per_device(train_grads, test_grads, precond):
    zl, y, core = lax.axis_index("zl"), lax.axis_index("y"), lax.axis_index("core")
    x, zh = lax.axis_index("x"), lax.axis_index("zh")
    count = test_grads.shape[0]
    width = train_grads.shape[0]

    even_y = jnp.mod(y + core, 2) == 0
    step_x, step_zh = first_step(x, core), first_step(zh, core)

    own = condition(test_grads, precond)
    line = [own] + [shift(own, "zl", k) for k in (1, 2, 3)]

    def partials(pieces):
        rows = jnp.concatenate(pieces, axis=0)
        rows = jnp.concatenate([rows, halve(rows, "y", True)], axis=0)
        rows = jnp.concatenate([rows, halve(rows, "y", False)], axis=0)
        both = [rows, lax.ppermute(rows, "core", [(0, 1), (1, 0)])]
        return [dot_t(r, train_grads).reshape(4, 2, count, width) for r in both]

    parts = [partials(line[:2]), partials(line[2:])]

    def block(home_x, home_zh):
        k = jnp.mod(zl - home_x, 4)
        d = jnp.mod(home_zh - y, 4)
        up = jnp.where(d < 2, d, 5 - d)
        down = jnp.where(d == 0, 0, jnp.where(d == 2, 3, jnp.where(d == 1, 2, 1)))
        m = [jnp.where(even_y, up, down), jnp.where(even_y, down, up)]
        found = [
            [
                lax.dynamic_slice(part[c], (m[c], jnp.mod(k, 2), 0, 0), (1, 1, count, width))[0, 0]
                for part in parts
            ]
            for c in range(2)
        ]
        return jnp.concatenate([jnp.where(k < 2, *f) for f in found], axis=0)

    def sum_x(homes):
        def blocks(home_x):
            return jnp.stack([block(home_x, home) for home in homes])

        send = jnp.stack([blocks(x + step_x), blocks(x + 2)])
        got = halve(send, "x", True).astype(jnp.float32)
        keep = blocks(x).astype(jnp.float32) + got[0]
        back = blocks(x - step_x).astype(jnp.float32) + got[1]
        return keep + halve(back.astype(jnp.bfloat16), "x", False).astype(jnp.float32)

    far = sum_x([zh + step_zh, zh + 2])
    near = sum_x([zh, zh - step_zh])
    near = near + halve(far.astype(jnp.bfloat16), "zh", True).astype(jnp.float32)
    last = halve(near[1].astype(jnp.bfloat16), "zh", False).astype(jnp.float32)
    scores = (near[0] + last).astype(jnp.bfloat16).reshape(2, count, width)
    scores = jnp.where(core == 0, scores, scores[::-1])
    return scores.reshape(2 * count, width)


def solution(mesh):
    fine = Mesh(mesh.devices.reshape(SIZES), AXES)
    train, col = ("zl", "y", "core"), ("x", "zh")
    return jax.shard_map(
        per_device,
        mesh=fine,
        in_specs=(P(train, col), P(train, col), P(col, None, None)),
        out_specs=P(col, train),
        check_vma=False,
    )
```

```python
import jax
import jax.numpy as jnp
from jax import lax
from jax.experimental import pallas as pl
from jax.experimental.pallas import tpu as pltpu
from jax.sharding import Mesh, PartitionSpec as P

AXES = ("zl", "y", "core", "x", "zh")
SIZES = (4, 4, 2, 4, 4)
BLOCK = 128


def condition_kernel(rows_ref, precond_ref, out_ref):
    for b in range(precond_ref.shape[0]):
        cols = pl.ds(b * BLOCK, BLOCK)
        out_ref[:, cols] = jnp.dot(
            rows_ref[:, cols], precond_ref[b], preferred_element_type=jnp.float32
        ).astype(out_ref.dtype)


def condition(rows, precond):
    return pl.pallas_call(
        condition_kernel,
        out_shape=jax.ShapeDtypeStruct(rows.shape, rows.dtype),
        in_specs=[pl.BlockSpec(memory_space=pltpu.VMEM)] * 2,
        out_specs=pl.BlockSpec(memory_space=pltpu.VMEM),
    )(rows, precond)


def shift(array, axis, step):
    size = SIZES[AXES.index(axis)]
    return lax.ppermute(array, axis, [(i, (i + step) % size) for i in range(size)])


def dot_t(rows, train):
    out = lax.dot_general(
        rows, train, (((1,), (1,)), ((), ())), preferred_element_type=jnp.float32
    )
    return out.astype(jnp.bfloat16)


def halve(array, axis, first):
    names = {"y": ("y", "core"), "x": ("core", "x"), "zh": ("core", "zh")}[axis]
    pairs = []
    for core in range(2):
        for i in range(4):
            up = (i + core + (0 if first else 1)) % 2 == 0
            to = (i + (1 if up else 3)) % 4
            if axis == "y":
                pairs.append((i * 2 + core, to * 2 + core))
            else:
                pairs.append((core * 4 + i, core * 4 + to))
    return lax.ppermute(array, names, pairs)


def first_step(index, core):
    return jnp.where(jnp.mod(index + core, 2) == 0, 1, 3)


def per_device(train_grads, test_grads, precond):
    zl, y, core = lax.axis_index("zl"), lax.axis_index("y"), lax.axis_index("core")
    x, zh = lax.axis_index("x"), lax.axis_index("zh")
    count = test_grads.shape[0]
    width = train_grads.shape[0]

    even_y = jnp.mod(y + core, 2) == 0
    step_x, step_zh = first_step(x, core), first_step(zh, core)

    own = condition(test_grads, precond)
    line = [own] + [shift(own, "zl", k) for k in (1, 2, 3)]

    def partials(pieces):
        rows = jnp.concatenate(pieces, axis=0)
        rows = jnp.concatenate([rows, halve(rows, "y", True)], axis=0)
        rows = jnp.concatenate([rows, halve(rows, "y", False)], axis=0)
        both = [rows, lax.ppermute(rows, "core", [(0, 1), (1, 0)])]
        return [dot_t(r, train_grads).reshape(4, 2, count, width) for r in both]

    parts = [partials(line[:2]), partials(line[2:])]

    def block(home_x, home_zh):
        k = jnp.mod(zl - home_x, 4)
        d = jnp.mod(home_zh - y, 4)
        up = jnp.where(d < 2, d, 5 - d)
        down = jnp.where(d == 0, 0, jnp.where(d == 2, 3, jnp.where(d == 1, 2, 1)))
        m = [jnp.where(even_y, up, down), jnp.where(even_y, down, up)]
        found = [
            [
                lax.dynamic_slice(part[c], (m[c], jnp.mod(k, 2), 0, 0), (1, 1, count, width))[0, 0]
                for part in parts
            ]
            for c in range(2)
        ]
        return jnp.concatenate([jnp.where(k < 2, *f) for f in found], axis=0)

    def sum_x(homes):
        def blocks(home_x):
            return jnp.stack([block(home_x, home) for home in homes])

        send = jnp.stack([blocks(x + step_x), blocks(x + 2)])
        got = halve(send, "x", True).astype(jnp.float32)
        keep = blocks(x).astype(jnp.float32) + got[0]
        back = blocks(x - step_x).astype(jnp.float32) + got[1]
        return keep + halve(back.astype(jnp.bfloat16), "x", False).astype(jnp.float32)

    far = sum_x([zh + step_zh, zh + 2])
    near = sum_x([zh, zh - step_zh])
    far = far.astype(jnp.bfloat16)
    back = near[1] + halve(far[1], "zh", True).astype(jnp.float32)
    last = halve(back.astype(jnp.bfloat16), "zh", False).astype(jnp.float32)
    ahead = halve(far[0], "zh", True).astype(jnp.float32)
    scores = (near[0] + ahead + last).astype(jnp.bfloat16).reshape(2, count, width)
    scores = jnp.where(core == 0, scores, scores[::-1])
    return scores.reshape(2 * count, width)


def solution(mesh):
    fine = Mesh(mesh.devices.reshape(SIZES), AXES)
    train, col = ("zl", "y", "core"), ("x", "zh")
    return jax.shard_map(
        per_device,
        mesh=fine,
        in_specs=(P(train, col), P(train, col), P(col, None, None)),
        out_specs=P(col, train),
        check_vma=False,
    )
```

```python
import jax
import jax.numpy as jnp
from jax import lax
from jax.experimental import pallas as pl
from jax.experimental.pallas import tpu as pltpu
from jax.sharding import Mesh, PartitionSpec as P

AXES = ("zl", "y", "core", "x", "zh")
SIZES = (4, 4, 2, 4, 4)
BLOCK = 128


def condition_kernel(rows_ref, precond_ref, out_ref):
    for b in range(precond_ref.shape[0]):
        cols = pl.ds(b * BLOCK, BLOCK)
        out_ref[:, cols] = jnp.dot(
            rows_ref[:, cols], precond_ref[b], preferred_element_type=jnp.float32
        ).astype(out_ref.dtype)


def condition(rows, precond):
    return pl.pallas_call(
        condition_kernel,
        out_shape=jax.ShapeDtypeStruct(rows.shape, rows.dtype),
        in_specs=[pl.BlockSpec(memory_space=pltpu.VMEM)] * 2,
        out_specs=pl.BlockSpec(memory_space=pltpu.VMEM),
        compiler_params=pltpu.CompilerParams(vmem_limit_bytes=8 * 1024 * 1024),
    )(rows, precond)


def shift(array, axis, step):
    size = SIZES[AXES.index(axis)]
    return lax.ppermute(array, axis, [(i, (i + step) % size) for i in range(size)])


def dot_t(rows, train):
    out = lax.dot_general(
        rows, train, (((1,), (1,)), ((), ())), preferred_element_type=jnp.float32
    )
    return out.astype(jnp.bfloat16)


def halve(array, axis, first):
    names = {"y": ("y", "core"), "x": ("core", "x"), "zh": ("core", "zh")}[axis]
    pairs = []
    for core in range(2):
        for i in range(4):
            up = (i + core + (0 if first else 1)) % 2 == 0
            to = (i + (1 if up else 3)) % 4
            if axis == "y":
                pairs.append((i * 2 + core, to * 2 + core))
            else:
                pairs.append((core * 4 + i, core * 4 + to))
    return lax.ppermute(array, names, pairs)


def first_step(index, core):
    return jnp.where(jnp.mod(index + core, 2) == 0, 1, 3)


def per_device(train_grads, test_grads, precond):
    zl, y, core = lax.axis_index("zl"), lax.axis_index("y"), lax.axis_index("core")
    x, zh = lax.axis_index("x"), lax.axis_index("zh")
    count = test_grads.shape[0]
    width = train_grads.shape[0]

    even_y = jnp.mod(y + core, 2) == 0
    step_x, step_zh = first_step(x, core), first_step(zh, core)

    own = condition(test_grads, precond)
    line = [own] + [shift(own, "zl", k) for k in (1, 2, 3)]

    def partials(pieces):
        rows = jnp.concatenate(pieces, axis=0)
        rows = jnp.concatenate([rows, halve(rows, "y", True)], axis=0)
        rows = jnp.concatenate([rows, halve(rows, "y", False)], axis=0)
        both = [rows, lax.ppermute(rows, "core", [(0, 1), (1, 0)])]
        return [dot_t(r, train_grads).reshape(4, 2, count, width) for r in both]

    parts = [partials(line[0::2]), partials(line[1::2])]

    def block(home_x, home_zh):
        k = jnp.mod(zl - home_x, 4)
        d = jnp.mod(home_zh - y, 4)
        up = jnp.where(d < 2, d, 5 - d)
        down = jnp.where(d == 0, 0, jnp.where(d == 2, 3, jnp.where(d == 1, 2, 1)))
        m = [jnp.where(even_y, up, down), jnp.where(even_y, down, up)]
        found = [
            [
                lax.dynamic_slice(part[c], (m[c], k // 2, 0, 0), (1, 1, count, width))[0, 0]
                for part in parts
            ]
            for c in range(2)
        ]
        return jnp.concatenate([jnp.where(jnp.mod(k, 2) == 0, *f) for f in found], axis=0)

    def sum_x(homes):
        def blocks(home_x):
            return jnp.stack([block(home_x, home) for home in homes])

        send = jnp.stack([blocks(x + step_x), blocks(x + 2)])
        got = halve(send, "x", True).astype(jnp.float32)
        keep = blocks(x).astype(jnp.float32) + got[0]
        back = blocks(x - step_x).astype(jnp.float32) + got[1]
        return keep + halve(back.astype(jnp.bfloat16), "x", False).astype(jnp.float32)

    far = sum_x([zh + step_zh, zh + 2])
    near = sum_x([zh, zh - step_zh])
    far = far.astype(jnp.bfloat16)
    back = near[1] + halve(far[1], "zh", True).astype(jnp.float32)
    last = halve(back.astype(jnp.bfloat16), "zh", False).astype(jnp.float32)
    ahead = halve(far[0], "zh", True).astype(jnp.float32)
    scores = (near[0] + ahead + last).astype(jnp.bfloat16).reshape(2, count, width)
    scores = jnp.where(core == 0, scores, scores[::-1])
    return scores.reshape(2 * count, width)


def solution(mesh):
    fine = Mesh(mesh.devices.reshape(SIZES), AXES)
    train, col = ("zl", "y", "core"), ("x", "zh")
    return jax.shard_map(
        per_device,
        mesh=fine,
        in_specs=(P(train, col), P(train, col), P(col, None, None)),
        out_specs=P(col, train),
        check_vma=False,
    )
```
